32 devices in a mesh: groups: 2 (over y), row: 8 (over z, x), col: 2 (over core).
Axes of the slice: x: 2, y: 2, z: 4, core: 2. Of those that a mesh axis runs over, the one named last changes fastest.
Arguments:
- states: bfloat16 [2, 32, 2, 8192], P(None, ('groups', 'row'), 'col'), parts along dimension 1, may hold values from -60 to 60
- norm_gain: float32 [2, 8192], P('col'), may hold values from 0.1 to 1.9
- w_query: bfloat16 [2, 2, 6144, 8192], P('col', None, 'row'), may hold values from -0.046875 to 0.046875
- w_key: bfloat16 [2, 2, 384, 8192], P('col', None, 'row'), may hold values from -0.046875 to 0.046875
- w_value: bfloat16 [2, 2, 384, 8192], P('col', None, 'row'), may hold values from -0.046875 to 0.046875
- w_out: bfloat16 [2, 2, 8192, 6144], P('col', None, 'row'), may hold values from -0.3125 to 0.3125
- key_cache: bfloat16 [32, 256, 6, 128], P(('groups', 'row'), None, 'col'), parts along dimension 0, may hold values from -260 to 260
- value_cache: bfloat16 [32, 256, 6, 128], P(('groups', 'row'), None, 'col'), parts along dimension 0, may hold values from -6 to 6
- cache_len: int32 [32], P(('groups', 'row')), parts along dimension 0, may hold values from 1 to 256, as said below
- slot_row: int32 [32], P('groups'), parts along dimension 0, may hold values from 0 to 15, each once
- exit_layer: int32 [2, 32], P(None, 'groups'), parts along dimension 1, may hold values from 0 to 125
Outputs:
- mixed: bfloat16 [2, 32, 2, 8192], P(None, 'groups', 'col', 'row'), parts along dimension 1
The draws below stay inside these ranges and needn't reach their ends.
There are 2 independent parts, one for each index of `groups`. The reference program is written for one: setup_inputs(seed, part) draws one part's arguments, and reference() takes and returns one part's arrays. A program takes and returns all parts, laid end to end along the dimension named above; an argument that names none is the same for every part. Nothing has to cross between parts.
Inputs may be any that keep to these rules, and one draw needn't show every extreme that they name: `cache_len`: some cache row is full in every draw. `slot_row`: each batch row appears once.
All inputs are finite; a program needn't handle non-finite values.
Results may differ from the reference program's by a relative error of at most 0.012.
The reference program's roundings to bfloat16 on the way count: a program that leaves them out, or rounds other values in their place, can miss the bound.
Values may be sent and summed in bfloat16 or wider, within the bound.
A program may use at most 128 MiB of HBM per device.

```python
import math
import jax
import jax.numpy as jnp
from jax import lax

D = 16384
HD = 128
QH = 96
KVH = 6
LAYERS = 126
LAYER_AT = 63
STEPS = 2
CACHE = 256
GROUP = 16
HALVES = 2
ROWS = 16


def draw_states(key, part):
    key = jax.random.fold_in(key, 11)
    first, second, third = jax.random.split(key, 3)
    shape = (STEPS, ROWS, HALVES, D // HALVES)
    base = jax.random.normal(first, shape, jnp.float32)
    row_scale = jnp.exp(jax.random.uniform(second, (STEPS, ROWS, 1, 1), jnp.float32) * math.log(10.0))
    feature = jnp.arange(D, dtype=jnp.float32).reshape(1, 1, HALVES, D // HALVES) / D
    col_scale = jnp.exp(feature * math.log(3.0)) * jnp.exp(jax.random.uniform(third, (1, 1, HALVES, D // HALVES), jnp.float32) * math.log(3.3))
    return jnp.clip(0.1 * base * row_scale * col_scale, -60.0, 60.0).astype(jnp.bfloat16)


def draw_key_cache(key, part):
    key = jax.random.fold_in(key, 23)
    first = jax.random.fold_in(key, 0)
    shape = (ROWS, CACHE, KVH, HD)
    keys = jnp.clip(jax.random.normal(first, shape, jnp.float32), -4.0, 4.0)
    return jnp.clip(keys, -260.0, 260.0).astype(jnp.bfloat16)


def draw_cache_len(key, part):
    key = jax.random.fold_in(key, 37)
    first, second = jax.random.split(key, 2)
    lengths = jax.random.randint(first, (ROWS,), 1, CACHE + 1)
    chosen = jax.random.randint(second, (), 0, ROWS)
    return jnp.where(jnp.arange(ROWS) == chosen, CACHE, lengths).astype(jnp.int32)


def with_ends(drawn, rng, low, top_value):
    longest = drawn.shape.index(max(drawn.shape))
    spots = []
    for shift in (0, 1):
        where = [jax.random.randint(jax.random.fold_in(rng, axis), (), 0, length) for axis, length in enumerate(drawn.shape)]
        where[longest] = (where[longest] + shift) % drawn.shape[longest]
        spots.append(tuple(where))
    return drawn.at[spots[0]].set(low).at[spots[1]].set(top_value)


def block_scale(rng, extent, shards, smallest, top_value):
    def one(axis_at, shards_of):
        steps = jax.random.uniform(jax.random.fold_in(jax.random.fold_in(rng, 6), axis_at), (shards_of,), jnp.float32, smallest / len(shards), top_value / len(shards))
        return jnp.repeat(jnp.exp(steps), extent[axis_at] // shards_of).reshape((-1,) + (1,) * (len(extent) - axis_at - 1))

    loudness = one(*shards[0])
    for cut in shards[1:]:
        loudness = loudness * one(*cut)
    return loudness


def normal_values(rng, dims, width, most, shards=(), kind=jnp.bfloat16):
    loudness = block_scale(rng, dims, shards, -0.22, 0.18) if shards else 1.0
    drawn = jax.random.normal(rng, dims, jnp.float32) * width * loudness
    return jnp.minimum(jnp.maximum(drawn, -most), most).astype(kind)


def setup_inputs(seed: int = 0, part: int = 0) -> dict:
    arg_keys = jax.random.split(jax.random.key(seed), 12)
    part_splits = jax.random.split(jax.random.fold_in(arg_keys[11], part), 12)
    states = draw_states(jax.random.fold_in(jax.random.fold_in(arg_keys[11], part), 71), part)
    norm_gain = jnp.clip(1.0 + 0.18 * jax.random.normal(arg_keys[1], (HALVES, D // HALVES), jnp.float32), 0.1, 1.9)
    w_query = normal_values(arg_keys[2], (HALVES, HALVES, QH // HALVES * HD, D // HALVES), D ** -0.5, 0.046875, ((0, 2), (2, 8)))
    w_key = normal_values(arg_keys[3], (HALVES, HALVES, KVH // HALVES * HD, D // HALVES), D ** -0.5, 0.046875, ((0, 2), (2, 8)))
    w_value = normal_values(arg_keys[4], (HALVES, HALVES, KVH // HALVES * HD, D // HALVES), D ** -0.5, 0.046875, ((0, 2), (2, 8)))
    w_out = normal_values(arg_keys[5], (HALVES, HALVES, D // HALVES, QH // HALVES * HD), (QH * HD // 32) ** -0.5, 0.3125, ((0, 2), (2, 8)))
    key_cache = draw_key_cache(jax.random.fold_in(jax.random.fold_in(arg_keys[11], part), 71), part)
    value_cache = normal_values(part_splits[7], (ROWS, CACHE, KVH, HD), 1.0, 6.0, ((0, 8), (2, 2)))
    cache_len = draw_cache_len(jax.random.fold_in(jax.random.fold_in(arg_keys[11], part), 71), part)
    slot_row = jax.random.permutation(part_splits[9], ROWS).astype(jnp.int32)
    exit_layer = with_ends(jax.random.randint(part_splits[10], (STEPS, ROWS), 0, LAYERS), jax.random.fold_in(part_splits[10], 1), 0, LAYERS - 1).astype(jnp.int32)
    return {"states": states, "norm_gain": norm_gain, "w_query": w_query, "w_key": w_key, "w_value": w_value, "w_out": w_out, "key_cache": key_cache, "value_cache": value_cache, "cache_len": cache_len, "slot_row": slot_row, "exit_layer": exit_layer}


epsilon = 1e-05

def reference(states, norm_gain, w_query, w_key, w_value, w_out, key_cache, value_cache, cache_len, slot_row, exit_layer):
    query_matrix = w_query.transpose(0, 3, 1, 2).reshape(D, QH * HD)
    key_matrix = w_key.transpose(0, 3, 1, 2).reshape(D, KVH * HD)
    value_matrix = w_value.transpose(0, 3, 1, 2).reshape(D, KVH * HD)
    out_matrix = w_out.transpose(0, 3, 1, 2).reshape(QH * HD, D)
    gain_vector = norm_gain.reshape(D).astype(jnp.float32)
    keys_cached = key_cache.astype(jnp.float32)
    values_cached = value_cache.astype(jnp.float32)
    valid_mask = jnp.arange(CACHE)[None, :] < cache_len[:, None]
    inverse = jnp.argsort(slot_row).astype(jnp.int32)
    scale_factor = HD ** (-0.5)
    new_keys = []
    new_values = []
    results = []
    for step_index in range(STEPS):
        hidden = states[step_index].reshape(ROWS, D).astype(jnp.float32)
        meansq = lax.optimization_barrier(jnp.mean(hidden * hidden, axis=1, keepdims=True))
        normed = (hidden * lax.rsqrt(meansq + epsilon) * gain_vector).astype(jnp.bfloat16)
        queries = jnp.dot(normed, query_matrix, preferred_element_type=jnp.float32).astype(jnp.bfloat16)[slot_row]
        keys_now = jnp.dot(normed, key_matrix, preferred_element_type=jnp.float32).astype(jnp.bfloat16)[slot_row]
        values_now = jnp.dot(normed, value_matrix, preferred_element_type=jnp.float32).astype(jnp.bfloat16)[slot_row]
        new_keys.append(keys_now.reshape(ROWS, KVH, HD).astype(jnp.float32))
        new_values.append(values_now.reshape(ROWS, KVH, HD).astype(jnp.float32))
        query_heads = queries.astype(jnp.float32).reshape(ROWS, KVH, GROUP, HD)
        cache_scores = jnp.einsum('bghd,blgd->bghl', query_heads, keys_cached) * scale_factor
        cache_scores = jnp.where(valid_mask[:, None, None, :], cache_scores, -jnp.inf)
        fresh_scores = jnp.stack([jnp.einsum('bghd,bgd->bgh', query_heads, earlier) for earlier in new_keys], axis=-1) * scale_factor
        largest = jnp.maximum(lax.optimization_barrier(jnp.max(cache_scores, axis=-1)), lax.optimization_barrier(jnp.max(fresh_scores, axis=-1)))
        cache_exps = jnp.exp(cache_scores - largest[..., None])
        fresh_exps = jnp.exp(fresh_scores - largest[..., None])
        denominator = lax.optimization_barrier(jnp.sum(cache_exps, axis=-1)) + lax.optimization_barrier(jnp.sum(fresh_exps, axis=-1))
        weights_cache = (cache_exps / denominator[..., None]).astype(jnp.bfloat16).astype(jnp.float32)
        weights_fresh = (fresh_exps / denominator[..., None]).astype(jnp.bfloat16).astype(jnp.float32)
        attended = jnp.einsum('bghl,blgd->bghd', weights_cache, values_cached)
        attended = attended + jnp.einsum('bght,btgd->bghd', weights_fresh, jnp.stack(new_values, axis=1))
        active = exit_layer[step_index][slot_row] > LAYER_AT
        attended = jnp.where(active[:, None, None, None], attended, 0.0).astype(jnp.bfloat16).reshape(ROWS, QH * HD)
        projected = jnp.dot(attended, out_matrix, preferred_element_type=jnp.float32)
        mixed = (hidden + projected[inverse]).astype(jnp.bfloat16)
        results.append(mixed.reshape(ROWS, HALVES, D // HALVES))
    return jnp.stack(results)
```

```python
import functools

import jax
import jax.numpy as jnp
from jax import lax
from jax.experimental import pallas as pl
from jax.experimental.pallas import tpu as pltpu
from jax.sharding import PartitionSpec as P

LAYER_AT = 63


epsilon = 1e-05


def on_device(
    states,
    norm_gain,
    w_query,
    w_key,
    w_value,
    w_out,
    key_cache,
    value_cache,
    cache_len,
    slot_row,
    exit_layer,
):
    row_count = lax.axis_size("row")
    row_index = lax.axis_index("row")
    own_rows = key_cache.shape[0]
    half_width = states.shape[3]
    model_width = half_width * w_query.shape[1]
    kv_local = key_cache.shape[2]
    head_size = key_cache.shape[3]
    group_size = w_query.shape[2] * row_count // (kv_local * head_size)
    piece_width = w_out.shape[2]
    scale_factor = head_size ** (-0.5)
    cache_slots = key_cache.shape[1]
    step_total = states.shape[0]
    valid_mask = jnp.arange(cache_slots)[None, :] < cache_len[:, None]
    own_slots = lax.dynamic_slice_in_dim(slot_row, row_index * own_rows, own_rows)
    gain_local = norm_gain[None]
    block_size = 1
    new_keys = []
    new_values = []
    results = []
    for first_step in range(0, step_total, block_size):
        block = states[first_step : first_step + block_size]
        gathered = lax.all_gather(block, "row", axis=1, tiled=True)
        widened = gathered.astype(jnp.float32)
        squares = jnp.sum(jnp.square(widened), axis=3)
        totals = lax.psum(squares, "col")
        scaling = lax.rsqrt(totals / model_width + epsilon)
        normed = (widened * scaling[..., None] * gain_local).astype(jnp.bfloat16)[:, :, 0, :]
        query_part = jnp.einsum(
            "srd,hcd->srhc", normed, w_query[0], preferred_element_type=jnp.float32
        )
        key_part = jnp.einsum("srd,hcd->srhc", normed, w_key[0], preferred_element_type=jnp.float32)
        value_part = jnp.einsum(
            "srd,hcd->srhc", normed, w_value[0], preferred_element_type=jnp.float32
        )
        query_sum, key_sum, value_sum = (
            lax.psum_scatter(query_part, "col", scatter_dimension=2, tiled=True),
            lax.psum_scatter(key_part, "col", scatter_dimension=2, tiled=True),
            lax.psum_scatter(value_part, "col", scatter_dimension=2, tiled=True),
        )
        query_sorted = jnp.take(query_sum.astype(jnp.bfloat16), slot_row, axis=1)
        key_sorted = jnp.take(key_sum.astype(jnp.bfloat16), slot_row, axis=1)
        value_sorted = jnp.take(value_sum.astype(jnp.bfloat16), slot_row, axis=1)
        query_own, key_own, value_own = (
            lax.all_to_all(query_sorted, "row", split_axis=1, concat_axis=3, tiled=True),
            lax.all_to_all(key_sorted, "row", split_axis=1, concat_axis=3, tiled=True),
            lax.all_to_all(value_sorted, "row", split_axis=1, concat_axis=3, tiled=True),
        )
        queries = query_own[0].reshape(own_rows, kv_local, group_size, head_size)
        new_keys.append(key_own[0].reshape(own_rows, kv_local, head_size))
        new_values.append(value_own[0].reshape(own_rows, kv_local, head_size))
        cache_scores = (
            jnp.einsum("bghd,blgd->bghl", queries, key_cache, preferred_element_type=jnp.float32)
            * scale_factor
        )
        cache_scores = jnp.where(valid_mask[:, None, None, :], cache_scores, -jnp.inf)
        fresh_scores = (
            jnp.stack(
                [
                    jnp.einsum(
                        "bghd,bgd->bgh", queries, earlier, preferred_element_type=jnp.float32
                    )
                    for earlier in new_keys
                ],
                axis=-1,
            )
            * scale_factor
        )
        largest = jnp.maximum(jnp.max(cache_scores, axis=-1), jnp.max(fresh_scores, axis=-1))
        cache_exps = jnp.exp(cache_scores - largest[..., None])
        fresh_exps = jnp.exp(fresh_scores - largest[..., None])
        denominator = jnp.sum(cache_exps, axis=-1) + jnp.sum(fresh_exps, axis=-1)
        weights_cache = (cache_exps / denominator[..., None]).astype(jnp.bfloat16)
        weights_fresh = (fresh_exps / denominator[..., None]).astype(jnp.bfloat16)
        attended = jnp.einsum(
            "bghl,blgd->bghd", weights_cache, value_cache, preferred_element_type=jnp.float32
        )
        attended = attended + jnp.einsum(
            "bght,btgd->bghd",
            weights_fresh,
            jnp.stack(new_values, axis=1),
            preferred_element_type=jnp.float32,
        )
        active = jnp.take(exit_layer[first_step], own_slots) > LAYER_AT
        attended = (
            jnp.where(active[:, None, None, None], attended, 0.0)
            .astype(jnp.bfloat16)
            .reshape(own_rows, -1)
        )
        attended_block = [attended]
        attended_all = jnp.stack(attended_block)
        projection_terms = jnp.einsum(
            "srf,hcf->srhc",
            lax.all_gather(attended_all, "row", axis=1, tiled=True),
            w_out[0],
            preferred_element_type=jnp.float32,
        )
        projected = lax.psum_scatter(projection_terms, "col", scatter_dimension=2, tiled=True)
        reordered = jnp.zeros_like(projected).at[:, slot_row].set(projected)
        residual = lax.dynamic_slice_in_dim(
            gathered, row_index * piece_width, piece_width, 3
        ).astype(jnp.float32)
        results.append((residual + reordered).astype(jnp.bfloat16))
    return jnp.concatenate(results, axis=0)


MESH = pl.DeviceIdType.MESH
LANES = 128
Q_CHUNKS = 4
NEG = float("-inf")


def nt_dot(a, b):
    return lax.dot_general(a, b, (((1,), (1,)), ((), ())), preferred_element_type=jnp.float32)


def nn_dot(a, b):
    return lax.dot_general(a, b, (((1,), (0,)), ((), ())), preferred_element_type=jnp.float32)


def fused_kernel(
    states,
    gain,
    w_query,
    w_key,
    w_value,
    w_out,
    key_cache,
    value_cache,
    cache_len,
    slot_row,
    exit_layer,
    out,
    gath,
    wq,
    wkv,
    wo,
    kc,
    vc,
    kext,
    vext,
    sums_own,
    sums_in,
    sums_all,
    norm32,
    normed,
    acc,
    acc_in,
    a2a_out,
    a2a_in,
    q32,
    ag,
    att,
    acc2,
    acc2_in,
    resid,
    perm_q,
    perm_a,
    spread,
    mask,
    own_sem,
    wq_sem,
    wo_sem,
    cache_sem,
    gs_sem,
    gr_sem,
    ss_sem,
    sr_sem,
    rs_sem,
    rr_sem,
    as_sem,
    ar_sem,
    hs_sem,
    hr_sem,
):
    me = lax.axis_index("row")
    col = lax.axis_index("col")
    other = 1 - col
    x = lax.rem(me, 2)
    z = lax.div(me, 2)
    beside = me + 1 - 2 * x
    along = [lax.rem(z + d, 4) * 2 + x for d in (1, 2, 3)]
    across = [lax.rem(z + d, 4) * 2 + 1 - x for d in (0, 1, 2, 3)]
    peers = [lax.rem(me + d, 8) for d in range(1, 8)]
    half_width = gath.shape[2]
    model_width = half_width * 2
    k_chunk = half_width // Q_CHUNKS
    q_width = wq.shape[1]
    kv_width = w_key.shape[2]
    out_width = wo.shape[1]
    kv_heads = kext.shape[0]
    slots = kc.shape[1]
    o_chunk = wo.shape[2] // kv_heads
    f32 = jnp.float32
    bf16 = jnp.bfloat16

    own = pltpu.make_async_copy(states, gath.at[me], own_sem)
    own.start()
    w_copies = []
    for c in range(Q_CHUNKS):
        cols = pl.ds(c * k_chunk, k_chunk)
        group = []
        for o in range(2):
            group.append((w_query.at[0, o, :, cols], wq.at[o, :, cols]))
            group.append((w_key.at[0, o, :, cols], wkv.at[pl.ds(o * LANES, kv_width), cols]))
            group.append(
                (w_value.at[0, o, :, cols], wkv.at[pl.ds(o * LANES + kv_width, kv_width), cols])
            )
        w_copies.append(
            [
                pltpu.make_async_copy(src, dst, wq_sem.at[c, i])
                for i, (src, dst) in enumerate(group)
            ]
        )
    o_copies = []
    for g in range(kv_heads):
        cols = pl.ds(g * o_chunk, o_chunk)
        o_copies.append(
            [
                pltpu.make_async_copy(w_out.at[0, o, :, cols], wo.at[o, :, cols], wo_sem.at[g, o])
                for o in range(2)
            ]
        )
    c_copies = [
        pltpu.make_async_copy(key_cache, kc, cache_sem.at[0]),
        pltpu.make_async_copy(value_cache, vc, cache_sem.at[1]),
    ]
    for copy in w_copies[0] + c_copies:
        copy.start()
    for group in w_copies[1:] + o_copies:
        for copy in group:
            copy.start()

    barrier = pltpu.get_barrier_semaphore()
    for peer in peers:
        pl.semaphore_signal(barrier, inc=1, device_id={"row": peer}, device_id_type=MESH)
    pl.semaphore_signal(barrier, inc=1, device_id={"col": other}, device_id_type=MESH)
    pl.semaphore_wait(barrier, 8)

    sends = []

    def push(src, dst, send_sem, recv_sem, where):
        copy = pltpu.make_async_remote_copy(
            src_ref=src,
            dst_ref=dst,
            send_sem=send_sem,
            recv_sem=recv_sem,
            device_id=where,
            device_id_type=MESH,
        )
        copy.start()
        sends.append(copy)

    def landed(ref, recv_sem):
        pltpu.make_async_remote_copy(
            src_ref=ref,
            dst_ref=ref,
            send_sem=own_sem,
            recv_sem=recv_sem,
            device_id={"row": beside},
            device_id_type=MESH,
        ).wait_recv()

    def spread_own(view, c, send_sem, recv_sem):
        push(view(me), view(me), send_sem.at[c, 0], recv_sem.at[c, me], {"row": beside})
        for i, peer in enumerate(along):
            push(view(me), view(me), send_sem.at[c, 1 + i], recv_sem.at[c, me], {"row": peer})

    def forward(view, c, send_sem, recv_sem):
        for i, peer in enumerate(along):
            landed(view(peer), recv_sem.at[c, peer])
            push(view(peer), view(peer), send_sem.at[c, 4 + i], recv_sem.at[c, peer], {"row": beside})

    def collect(view, c, recv_sem):
        for peer in across:
            landed(view(peer), recv_sem.at[c, peer])

    def state_view(c):
        return lambda peer: gath.at[peer, :, pl.ds(c * k_chunk, k_chunk)]

    own.wait()
    for c in range(Q_CHUNKS):
        spread_own(state_view(c), c, gs_sem, gr_sem)

    mine = gath[me].astype(f32)
    square = jnp.sum(mine * mine, axis=1, keepdims=True)
    sums_own[0:4, :] = jnp.broadcast_to(square, (4, LANES))
    sums_own[4:8, :] = jnp.zeros((4, LANES), f32)
    push(sums_own, sums_in, ss_sem.at[0], sr_sem.at[8], {"col": other})
    landed(sums_in, sr_sem.at[8])
    sums_all[me] = sums_own[...] + sums_in[...]
    for i, peer in enumerate(peers):
        push(sums_all.at[me], sums_all.at[me], ss_sem.at[1 + i], sr_sem.at[me], {"row": peer})

    for o in range(2):
        wkv[pl.ds(o * LANES + 2 * kv_width, LANES - 2 * kv_width), :] = jnp.zeros(
            (LANES - 2 * kv_width, half_width), bf16
        )
    r = lax.broadcasted_iota(jnp.int32, (256, 1), 0)
    slot_of = (r >> 5) * 2 + (r & 1)
    target = jnp.zeros((256, 1), jnp.int32)
    for t in range(16):
        target = jnp.where(slot_of == t, slot_row[t], target)
    q = lax.broadcasted_iota(jnp.int32, (256, 256), 1)
    row_of = ((q >> 2) & 7) * 2 + (q & 1)
    hit = (((r >> 2) & 7) == (q >> 5)) & (((r >> 1) & 1) == ((q >> 1) & 1)) & (row_of == target)
    perm_q[...] = jnp.where(hit, 1.0, 0.0).astype(bf16)
    q = lax.broadcasted_iota(jnp.int32, (1, 256), 1)
    slot_of = (q >> 5) * 2 + (q & 1)
    target = jnp.zeros((1, 256), jnp.int32)
    for t in range(16):
        target = jnp.where(slot_of == t, slot_row[t], target)
    r = lax.broadcasted_iota(jnp.int32, (256, 256), 0)
    hit = (((q >> 2) & 7) == (r >> 5)) & (((q >> 1) & 1) == ((r >> 4) & 1)) & ((r & 15) == target)
    perm_a[...] = jnp.where(hit, 1.0, 0.0).astype(bf16)
    n = lax.broadcasted_iota(jnp.int32, (LANES, 6 * LANES), 1)
    lane = lax.broadcasted_iota(jnp.int32, (LANES, 6 * LANES), 0)
    place = jnp.where(lane < kv_width, lane, lane - kv_width + 3 * LANES)
    place = jnp.where(lane < 2 * kv_width, place, -10000)
    for p in range(8):
        spread[p * LANES : (p + 1) * LANES, :] = jnp.where(
            n == place + p * kv_width, 1.0, 0.0
        ).astype(bf16)
    r = lax.broadcasted_iota(jnp.int32, mask.shape, 0)
    k = lax.broadcasted_iota(jnp.int32, mask.shape, 1)
    b = r & 1
    s = (r >> 1) & 1
    f = k - 2 * slots - 8
    limit = b * slots + jnp.where(b == 0, cache_len[0], cache_len[1])
    cached = (k >= b * slots) & (k < limit)
    fresh = (f >= 0) & (f < 4) & ((f & 1) == b) & ((f >> 1) <= s)
    mask[...] = jnp.where(cached | fresh, 0.0, NEG)
    r = lax.broadcasted_iota(jnp.int32, (64, LANES), 0) & 3
    exits = jnp.zeros((64, LANES), jnp.int32)
    for step in range(2):
        for slot in range(2):
            layer = exit_layer[step, slot_row[me * 2 + slot]]
            exits = jnp.where(r == step * 2 + slot, layer, exits)

    def stage_caches():
        for copy in c_copies:
            copy.wait()
        for slot in range(2):
            for g in range(kv_heads):
                kext[g, slot * slots : (slot + 1) * slots, :] = kc[slot, :, g, :]
                vext[g, slot * slots : (slot + 1) * slots, :] = vc[slot, :, g, :]
        for g in range(kv_heads):
            kext[g, 2 * slots :, :] = jnp.zeros((LANES, LANES), bf16)
            vext[g, 2 * slots :, :] = jnp.zeros((LANES, LANES), bf16)

    forward(state_view(0), 0, gs_sem, gr_sem)
    stage_caches()
    for peer in peers:
        landed(sums_all.at[peer], sr_sem.at[peer])
    scale = [
        lax.rsqrt(sums_all[p, 0:4, 0:1] / model_width + epsilon) for p in range(8)
    ]
    for c in range(Q_CHUNKS):
        cols = pl.ds(c * k_chunk, k_chunk)
        if c + 1 < Q_CHUNKS:
            forward(state_view(c + 1), c + 1, gs_sem, gr_sem)
        collect(state_view(c), c, gr_sem)
        for p in range(8):
            norm32[p * 4 : (p + 1) * 4, :] = (
                gath[p, :, cols].astype(f32) * scale[p] * gain[:, cols]
            )
        normed[...] = norm32[...].astype(bf16)
        for copy in w_copies[c]:
            copy.wait()

        kv = nt_dot(normed[...], wkv[:, cols])
        for o in range(2):
            part = kv[:, o * LANES : (o + 1) * LANES]
            if c == 0:
                acc[o, :, q_width:] = part
            else:
                acc[o, :, q_width:] += part

        def query_tiles(half, c=c, cols=cols):
            @pl.loop(0, q_width // 256)
            def _(i):
                at = pl.ds(pl.multiple_of(i * 256, 256), 256)
                part = nt_dot(normed[...], wq[half, at, cols])
                if c == 0:
                    acc[half, :, at] = part
                else:
                    acc[half, :, at] += part

        query_tiles(other)
        if c == Q_CHUNKS - 1:
            push(acc.at[other], acc_in, rs_sem.at[0], rr_sem.at[0], {"col": other})
        query_tiles(col)

    for p in range(8):
        piece = gath[p, :, pl.ds(pl.multiple_of(me * out_width, out_width), out_width)].astype(f32)
        for step in range(2):
            resid[step * 16 + p * 2 : step * 16 + p * 2 + 2, :] = piece[step * 2 : step * 2 + 2]

    landed(acc_in, rr_sem.at[0])
    total = (acc[col] + acc_in[...]).astype(bf16)
    stack = [total[:, j * LANES : (j + 1) * LANES] for j in range(7)]
    stack.append(jnp.zeros((32, LANES), bf16))
    a2a_out[...] = nn_dot(perm_q[...], jnp.concatenate(stack, axis=0)).astype(bf16)
    for i, peer in enumerate(peers):
        push(
            a2a_out.at[pl.ds(pl.multiple_of(peer * 32, 32), 32), :],
            a2a_in.at[me],
            as_sem.at[i],
            ar_sem.at[me],
            {"row": peer},
        )
    a2a_in[me] = a2a_out[pl.ds(pl.multiple_of(me * 32, 32), 32), :]
    for peer in peers:
        landed(a2a_in.at[peer], ar_sem.at[peer])

    news = jnp.concatenate([a2a_in[p, 16:32, :] for p in range(8)], axis=1)
    news = nn_dot(news, spread[...]).astype(bf16)
    for g in range(kv_heads):
        kext[g, 2 * slots : 2 * slots + 16, :] = news[:, g * LANES : (g + 1) * LANES]
        vext[g, 2 * slots : 2 * slots + 16, :] = news[
            :, (kv_heads + g) * LANES : (kv_heads + g + 1) * LANES
        ]
    for p in range(8):
        q32[p * 24 : (p + 1) * 24, :] = a2a_in[p].astype(f32)[0:24]

    def heads_view(g):
        return lambda peer: ag.at[peer, pl.ds(g * 64, 64), :]

    for g in range(kv_heads):
        scores = nt_dot(q32[g * 64 : (g + 1) * 64, :].astype(bf16), kext[g]) * (LANES ** -0.5)
        scores = scores + mask[...]
        exps = jnp.exp(scores - jnp.max(scores, axis=1, keepdims=True))
        probs = (exps / jnp.sum(exps, axis=1, keepdims=True)).astype(bf16)
        result = nn_dot(probs, vext[g])
        result = jnp.where(exits > LAYER_AT, result, 0.0)
        ag[me, g * 64 : (g + 1) * 64, :] = result.astype(bf16)
        spread_own(heads_view(g), g, hs_sem, hr_sem)

    forward(heads_view(0), 0, hs_sem, hr_sem)
    for g in range(kv_heads):
        if g + 1 < kv_heads:
            forward(heads_view(g + 1), g + 1, hs_sem, hr_sem)
        collect(heads_view(g), g, hr_sem)
        for block in range(2):
            at = g * 64 + block * 32
            rows = ag[:, at : at + 32, :].reshape(256, LANES)
            tiles = nn_dot(perm_a[...], rows).astype(bf16)
            for j in range(8):
                lanes = (block * 8 + j) * LANES
                att[:, lanes : lanes + LANES] = tiles[j * 32 : (j + 1) * 32, :]
        for copy in o_copies[g]:
            copy.wait()

        def out_tiles(half, g=g):
            @pl.loop(0, out_width // 256)
            def _(i):
                at = pl.ds(pl.multiple_of(i * 256, 256), 256)
                part = nt_dot(att[...], wo[half, at, pl.ds(g * o_chunk, o_chunk)])
                if g == 0:
                    acc2[half, :, at] = part
                else:
                    acc2[half, :, at] += part

        out_tiles(other)
        if g == kv_heads - 1:
            push(acc2.at[other], acc2_in, rs_sem.at[1], rr_sem.at[1], {"col": other})
        out_tiles(col)
    resid[...] += acc2[col]
    landed(acc2_in, rr_sem.at[1])
    final = (resid[...] + acc2_in[...]).astype(bf16)
    for step in range(2):
        out[step] = final[step * 16 : (step + 1) * 16, :]
    for copy in sends:
        copy.wait_send()


def fused(
    states,
    norm_gain,
    w_query,
    w_key,
    w_value,
    w_out,
    key_cache,
    value_cache,
    cache_len,
    slot_row,
    exit_layer,
):
    steps, own_rows, _, half_width = states.shape
    kv_heads = key_cache.shape[2]
    slots = key_cache.shape[1]
    q_width = w_query.shape[2]
    out_width = w_out.shape[2]
    head_width = w_out.shape[3]
    any_space = pl.BlockSpec(memory_space=pl.ANY)
    vmem = pl.BlockSpec(memory_space=pltpu.VMEM)
    smem = pl.BlockSpec(memory_space=pltpu.SMEM)
    f32 = jnp.float32
    bf16 = jnp.bfloat16
    keys = 2 * slots + LANES
    dma = pltpu.SemaphoreType.DMA
    result = pl.pallas_call(
        fused_kernel,
        out_shape=jax.ShapeDtypeStruct((steps, 16, out_width), bf16),
        in_specs=[any_space, vmem] + [any_space] * 6 + [smem] * 3,
        out_specs=vmem,
        scratch_shapes=[
            pltpu.VMEM((8, steps * own_rows, half_width), bf16),
            pltpu.VMEM((2, q_width, half_width), bf16),
            pltpu.VMEM((2 * LANES, half_width), bf16),
            pltpu.VMEM((2, out_width, head_width), bf16),
            pltpu.VMEM(key_cache.shape, bf16),
            pltpu.VMEM(value_cache.shape, bf16),
            pltpu.VMEM((kv_heads, keys, LANES), bf16),
            pltpu.VMEM((kv_heads, keys, LANES), bf16),
            pltpu.VMEM((8, LANES), f32),
            pltpu.VMEM((8, LANES), f32),
            pltpu.VMEM((8, 8, LANES), f32),
            pltpu.VMEM((32, half_width // Q_CHUNKS), f32),
            pltpu.VMEM((32, half_width // Q_CHUNKS), bf16),
            pltpu.VMEM((2, 32, q_width + LANES), f32),
            pltpu.VMEM((32, q_width + LANES), f32),
            pltpu.VMEM((256, LANES), bf16),
            pltpu.VMEM((8, 32, LANES), bf16),
            pltpu.VMEM((192, LANES), f32),
            pltpu.VMEM((8, 192, LANES), bf16),
            pltpu.VMEM((32, head_width // kv_heads), bf16),
            pltpu.VMEM((2, 32, out_width), f32),
            pltpu.VMEM((32, out_width), f32),
            pltpu.VMEM((32, out_width), f32),
            pltpu.VMEM((256, 256), bf16),
            pltpu.VMEM((256, 256), bf16),
            pltpu.VMEM((8 * LANES, 6 * LANES), bf16),
            pltpu.VMEM((64, keys), f32),
            dma,
            dma((Q_CHUNKS, 6)),
            dma((kv_heads, 2)),
            dma((2,)),
            dma((Q_CHUNKS, 7)),
            dma((Q_CHUNKS, 8)),
            dma((8,)),
            dma((9,)),
            dma((2,)),
            dma((2,)),
            dma((7,)),
            dma((8,)),
            dma((kv_heads, 7)),
            dma((kv_heads, 8)),
        ],
        compiler_params=pltpu.CompilerParams(
            collective_id=0, has_side_effects=True, vmem_limit_bytes=63 * 1024 * 1024
        ),
        name="fused_layer",
    )(
        states.reshape(steps * own_rows, half_width),
        norm_gain,
        w_query,
        w_key,
        w_value,
        w_out,
        key_cache,
        value_cache,
        cache_len,
        slot_row,
        exit_layer,
    )
    return result[:, :, None, :]


def on_device_any(*args):
    states, _, w_query, w_key, _, w_out, key_cache = args[:7]
    fits = (
        lax.axis_size("row") == 8
        and lax.axis_size("col") == 2
        and states.shape[:2] == (2, 2)
        and w_query.shape[1:3] == (2, 6 * LANES)
        and w_key.shape[2] == 48
        and key_cache.shape[2:] == (3, LANES)
        and w_out.shape[3] == 48 * LANES
    )
    return fused(*args) if fits else on_device(*args)


def solution(mesh):
    return jax.shard_map(
        on_device_any,
        mesh=mesh,
        in_specs=(
            P(None, ("groups", "row"), "col", None),
            P("col", None),
            P("col", None, "row", None),
            P("col", None, "row", None),
            P("col", None, "row", None),
            P("col", None, "row", None),
            P(("groups", "row"), None, "col", None),
            P(("groups", "row"), None, "col", None),
            P(("groups", "row")),
            P("groups"),
            P(None, "groups"),
        ),
        out_specs=P(None, "groups", "col", "row"),
        check_vma=False,
    )
```

```python
import functools

import jax
import jax.numpy as jnp
from jax import lax
from jax.experimental import pallas as pl
from jax.experimental.pallas import tpu as pltpu
from jax.sharding import PartitionSpec as P

LAYER_AT = 63


epsilon = 1e-05


def on_device(
    states,
    norm_gain,
    w_query,
    w_key,
    w_value,
    w_out,
    key_cache,
    value_cache,
    cache_len,
    slot_row,
    exit_layer,
):
    row_count = lax.axis_size("row")
    row_index = lax.axis_index("row")
    own_rows = key_cache.shape[0]
    half_width = states.shape[3]
    model_width = half_width * w_query.shape[1]
    kv_local = key_cache.shape[2]
    head_size = key_cache.shape[3]
    group_size = w_query.shape[2] * row_count // (kv_local * head_size)
    piece_width = w_out.shape[2]
    scale_factor = head_size ** (-0.5)
    cache_slots = key_cache.shape[1]
    step_total = states.shape[0]
    valid_mask = jnp.arange(cache_slots)[None, :] < cache_len[:, None]
    own_slots = lax.dynamic_slice_in_dim(slot_row, row_index * own_rows, own_rows)
    gain_local = norm_gain[None]
    block_size = 1
    new_keys = []
    new_values = []
    results = []
    for first_step in range(0, step_total, block_size):
        block = states[first_step : first_step + block_size]
        gathered = lax.all_gather(block, "row", axis=1, tiled=True)
        widened = gathered.astype(jnp.float32)
        squares = jnp.sum(jnp.square(widened), axis=3)
        totals = lax.psum(squares, "col")
        scaling = lax.rsqrt(totals / model_width + epsilon)
        normed = (widened * scaling[..., None] * gain_local).astype(jnp.bfloat16)[:, :, 0, :]
        query_part = jnp.einsum(
            "srd,hcd->srhc", normed, w_query[0], preferred_element_type=jnp.float32
        )
        key_part = jnp.einsum("srd,hcd->srhc", normed, w_key[0], preferred_element_type=jnp.float32)
        value_part = jnp.einsum(
            "srd,hcd->srhc", normed, w_value[0], preferred_element_type=jnp.float32
        )
        query_sum, key_sum, value_sum = (
            lax.psum_scatter(query_part, "col", scatter_dimension=2, tiled=True),
            lax.psum_scatter(key_part, "col", scatter_dimension=2, tiled=True),
            lax.psum_scatter(value_part, "col", scatter_dimension=2, tiled=True),
        )
        query_sorted = jnp.take(query_sum.astype(jnp.bfloat16), slot_row, axis=1)
        key_sorted = jnp.take(key_sum.astype(jnp.bfloat16), slot_row, axis=1)
        value_sorted = jnp.take(value_sum.astype(jnp.bfloat16), slot_row, axis=1)
        query_own, key_own, value_own = (
            lax.all_to_all(query_sorted, "row", split_axis=1, concat_axis=3, tiled=True),
            lax.all_to_all(key_sorted, "row", split_axis=1, concat_axis=3, tiled=True),
            lax.all_to_all(value_sorted, "row", split_axis=1, concat_axis=3, tiled=True),
        )
        queries = query_own[0].reshape(own_rows, kv_local, group_size, head_size)
        new_keys.append(key_own[0].reshape(own_rows, kv_local, head_size))
        new_values.append(value_own[0].reshape(own_rows, kv_local, head_size))
        cache_scores = (
            jnp.einsum("bghd,blgd->bghl", queries, key_cache, preferred_element_type=jnp.float32)
            * scale_factor
        )
        cache_scores = jnp.where(valid_mask[:, None, None, :], cache_scores, -jnp.inf)
        fresh_scores = (
            jnp.stack(
                [
                    jnp.einsum(
                        "bghd,bgd->bgh", queries, earlier, preferred_element_type=jnp.float32
                    )
                    for earlier in new_keys
                ],
                axis=-1,
            )
            * scale_factor
        )
        largest = jnp.maximum(jnp.max(cache_scores, axis=-1), jnp.max(fresh_scores, axis=-1))
        cache_exps = jnp.exp(cache_scores - largest[..., None])
        fresh_exps = jnp.exp(fresh_scores - largest[..., None])
        denominator = jnp.sum(cache_exps, axis=-1) + jnp.sum(fresh_exps, axis=-1)
        weights_cache = (cache_exps / denominator[..., None]).astype(jnp.bfloat16)
        weights_fresh = (fresh_exps / denominator[..., None]).astype(jnp.bfloat16)
        attended = jnp.einsum(
            "bghl,blgd->bghd", weights_cache, value_cache, preferred_element_type=jnp.float32
        )
        attended = attended + jnp.einsum(
            "bght,btgd->bghd",
            weights_fresh,
            jnp.stack(new_values, axis=1),
            preferred_element_type=jnp.float32,
        )
        active = jnp.take(exit_layer[first_step], own_slots) > LAYER_AT
        attended = (
            jnp.where(active[:, None, None, None], attended, 0.0)
            .astype(jnp.bfloat16)
            .reshape(own_rows, -1)
        )
        attended_block = [attended]
        attended_all = jnp.stack(attended_block)
        projection_terms = jnp.einsum(
            "srf,hcf->srhc",
            lax.all_gather(attended_all, "row", axis=1, tiled=True),
            w_out[0],
            preferred_element_type=jnp.float32,
        )
        projected = lax.psum_scatter(projection_terms, "col", scatter_dimension=2, tiled=True)
        reordered = jnp.zeros_like(projected).at[:, slot_row].set(projected)
        residual = lax.dynamic_slice_in_dim(
            gathered, row_index * piece_width, piece_width, 3
        ).astype(jnp.float32)
        results.append((residual + reordered).astype(jnp.bfloat16))
    return jnp.concatenate(results, axis=0)


MESH = pl.DeviceIdType.MESH
LANES = 128
Q_CHUNKS = 4
NEG = float("-inf")


def nt_dot(a, b):
    return lax.dot_general(a, b, (((1,), (1,)), ((), ())), preferred_element_type=jnp.float32)


def nn_dot(a, b):
    return lax.dot_general(a, b, (((1,), (0,)), ((), ())), preferred_element_type=jnp.float32)


def fused_kernel(
    states,
    gain,
    w_query,
    w_key,
    w_value,
    w_out,
    key_cache,
    value_cache,
    cache_len,
    slot_row,
    exit_layer,
    out,
    gath,
    wq,
    wkv,
    wo,
    kc,
    vc,
    kext,
    vext,
    sums_own,
    sums_in,
    sums_all,
    own_rows,
    own32,
    norm32,
    normed,
    acc,
    acc_in,
    a2a_out,
    a2a_in,
    q32,
    ag,
    att,
    acc2,
    acc2_in,
    resid,
    perm_q,
    perm_a,
    spread,
    mask,
    own_sem,
    wq_sem,
    wo_sem,
    cache_sem,
    gs_sem,
    gr_sem,
    ss_sem,
    sr_sem,
    rs_sem,
    rr_sem,
    as_sem,
    ar_sem,
    hs_sem,
    hr_sem,
):
    me = lax.axis_index("row")
    col = lax.axis_index("col")
    other = 1 - col
    x = lax.rem(me, 2)
    z = lax.div(me, 2)
    beside = me + 1 - 2 * x
    along = [lax.rem(z + d, 4) * 2 + x for d in (1, 2, 3)]
    across = [lax.rem(z + d, 4) * 2 + 1 - x for d in (0, 1, 2, 3)]
    peers = [lax.rem(me + d, 8) for d in range(1, 8)]
    half_width = gath.shape[2]
    model_width = half_width * 2
    k_chunk = half_width // Q_CHUNKS
    q_width = wq.shape[1]
    kv_width = w_key.shape[2]
    out_width = wo.shape[1]
    kv_heads = kext.shape[0]
    slots = kc.shape[2]
    o_chunk = wo.shape[2] // kv_heads
    f32 = jnp.float32
    bf16 = jnp.bfloat16

    own = pltpu.make_async_copy(states, own_rows, own_sem)
    own.start()
    w_copies = []
    for c in range(Q_CHUNKS):
        cols = pl.ds(c * k_chunk, k_chunk)
        group = []
        for o in range(2):
            group.append((w_query.at[0, o, :, cols], wq.at[o, :, cols]))
            group.append((w_key.at[0, o, :, cols], wkv.at[pl.ds(o * LANES, kv_width), cols]))
            group.append(
                (w_value.at[0, o, :, cols], wkv.at[pl.ds(o * LANES + kv_width, kv_width), cols])
            )
        w_copies.append(
            [
                pltpu.make_async_copy(src, dst, wq_sem.at[c, i])
                for i, (src, dst) in enumerate(group)
            ]
        )
    o_copies = []
    for g in range(kv_heads):
        cols = pl.ds(g * o_chunk, o_chunk)
        o_copies.append(
            [
                pltpu.make_async_copy(w_out.at[0, o, :, cols], wo.at[o, :, cols], wo_sem.at[g, o])
                for o in range(2)
            ]
        )
    c_copies = [
        pltpu.make_async_copy(key_cache, kc, cache_sem.at[0]),
        pltpu.make_async_copy(value_cache, vc, cache_sem.at[1]),
    ]
    for copy in w_copies[0] + c_copies:
        copy.start()
    for group in w_copies[1:] + o_copies:
        for copy in group:
            copy.start()

    barrier = pltpu.get_barrier_semaphore()
    for peer in peers:
        pl.semaphore_signal(barrier, inc=1, device_id={"row": peer}, device_id_type=MESH)
    pl.semaphore_signal(barrier, inc=1, device_id={"col": other}, device_id_type=MESH)
    pl.semaphore_wait(barrier, 8)

    sends = []

    def push(src, dst, send_sem, recv_sem, where):
        copy = pltpu.make_async_remote_copy(
            src_ref=src,
            dst_ref=dst,
            send_sem=send_sem,
            recv_sem=recv_sem,
            device_id=where,
            device_id_type=MESH,
        )
        copy.start()
        sends.append(copy)

    def landed(ref, recv_sem):
        pltpu.make_async_remote_copy(
            src_ref=ref,
            dst_ref=ref,
            send_sem=own_sem,
            recv_sem=recv_sem,
            device_id={"row": beside},
            device_id_type=MESH,
        ).wait_recv()

    def spread_own(view, c, send_sem, recv_sem):
        push(view(me), view(me), send_sem.at[c, 0], recv_sem.at[c, me], {"row": beside})
        for i, peer in enumerate(along):
            push(view(me), view(me), send_sem.at[c, 1 + i], recv_sem.at[c, me], {"row": peer})

    def forward(view, c, send_sem, recv_sem):
        for i, peer in enumerate(along):
            landed(view(peer), recv_sem.at[c, peer])
            push(view(peer), view(peer), send_sem.at[c, 4 + i], recv_sem.at[c, peer], {"row": beside})

    def collect(view, c, recv_sem):
        for peer in across:
            landed(view(peer), recv_sem.at[c, peer])

    def state_view(c):
        return lambda peer: gath.at[peer, :, pl.ds(c * k_chunk, k_chunk)]

    own.wait()
    for step in range(2):
        own32[step * 2 : step * 2 + 2, :] = own_rows[step].astype(f32)
    gath[me] = own32[...].astype(bf16)
    for c in range(Q_CHUNKS):
        spread_own(state_view(c), c, gs_sem, gr_sem)

    mine = own32[...]
    square = jnp.sum(mine * mine, axis=1, keepdims=True)
    sums_own[0:4, :] = jnp.broadcast_to(square, (4, LANES))
    sums_own[4:8, :] = jnp.zeros((4, LANES), f32)
    push(sums_own, sums_in, ss_sem.at[0], sr_sem.at[8], {"col": other})
    landed(sums_in, sr_sem.at[8])
    sums_all[me] = sums_own[...] + sums_in[...]
    for i, peer in enumerate(peers):
        push(sums_all.at[me], sums_all.at[me], ss_sem.at[1 + i], sr_sem.at[me], {"row": peer})

    for o in range(2):
        wkv[pl.ds(o * LANES + 2 * kv_width, LANES - 2 * kv_width), :] = jnp.zeros(
            (LANES - 2 * kv_width, half_width), bf16
        )
    r = lax.broadcasted_iota(jnp.int32, (256, 1), 0)
    slot_of = (r >> 5) * 2 + (r & 1)
    target = jnp.zeros((256, 1), jnp.int32)
    for t in range(16):
        target = jnp.where(slot_of == t, slot_row[t], target)
    q = lax.broadcasted_iota(jnp.int32, (256, 256), 1)
    row_of = ((q >> 2) & 7) * 2 + (q & 1)
    hit = (((r >> 2) & 7) == (q >> 5)) & (((r >> 1) & 1) == ((q >> 1) & 1)) & (row_of == target)
    perm_q[...] = jnp.where(hit, 1.0, 0.0).astype(bf16)
    q = lax.broadcasted_iota(jnp.int32, (1, 256), 1)
    slot_of = (q >> 5) * 2 + (q & 1)
    target = jnp.zeros((1, 256), jnp.int32)
    for t in range(16):
        target = jnp.where(slot_of == t, slot_row[t], target)
    r = lax.broadcasted_iota(jnp.int32, (256, 256), 0)
    hit = (((q >> 2) & 7) == (r >> 5)) & (((q >> 1) & 1) == ((r >> 4) & 1)) & ((r & 15) == target)
    perm_a[...] = jnp.where(hit, 1.0, 0.0).astype(bf16)
    n = lax.broadcasted_iota(jnp.int32, (LANES, 6 * LANES), 1)
    lane = lax.broadcasted_iota(jnp.int32, (LANES, 6 * LANES), 0)
    place = jnp.where(lane < kv_width, lane, lane - kv_width + 3 * LANES)
    place = jnp.where(lane < 2 * kv_width, place, -10000)
    for p in range(8):
        spread[p * LANES : (p + 1) * LANES, :] = jnp.where(
            n == place + p * kv_width, 1.0, 0.0
        ).astype(bf16)
    r = lax.broadcasted_iota(jnp.int32, mask.shape, 0)
    k = lax.broadcasted_iota(jnp.int32, mask.shape, 1)
    b = r & 1
    s = (r >> 1) & 1
    f = k - 2 * slots - 8
    limit = b * slots + jnp.where(b == 0, cache_len[0], cache_len[1])
    cached = (k >= b * slots) & (k < limit)
    fresh = (f >= 0) & (f < 4) & ((f & 1) == b) & ((f >> 1) <= s)
    mask[...] = jnp.where(cached | fresh, 0.0, NEG)
    r = lax.broadcasted_iota(jnp.int32, (64, LANES), 0) & 3
    exits = jnp.zeros((64, LANES), jnp.int32)
    for step in range(2):
        for slot in range(2):
            layer = exit_layer[step, slot_row[me * 2 + slot]]
            exits = jnp.where(r == step * 2 + slot, layer, exits)

    def stage_caches():
        for copy in c_copies:
            copy.wait()
        for slot in range(2):
            for g in range(kv_heads):
                kext[g, slot * slots : (slot + 1) * slots, :] = kc[slot, g]
                vext[g, slot * slots : (slot + 1) * slots, :] = vc[slot, g]
        for g in range(kv_heads):
            kext[g, 2 * slots :, :] = jnp.zeros((LANES, LANES), bf16)
            vext[g, 2 * slots :, :] = jnp.zeros((LANES, LANES), bf16)

    forward(state_view(0), 0, gs_sem, gr_sem)
    stage_caches()
    for peer in peers:
        landed(sums_all.at[peer], sr_sem.at[peer])
    scale = [
        lax.rsqrt(sums_all[p, 0:4, 0:1] / model_width + epsilon) for p in range(8)
    ]
    for c in range(Q_CHUNKS):
        cols = pl.ds(c * k_chunk, k_chunk)
        if c + 1 < Q_CHUNKS:
            forward(state_view(c + 1), c + 1, gs_sem, gr_sem)
        collect(state_view(c), c, gr_sem)
        for p in range(8):
            norm32[p * 4 : (p + 1) * 4, :] = (
                gath[p, :, cols].astype(f32) * scale[p] * gain[:, cols]
            )
        normed[...] = norm32[...].astype(bf16)
        for copy in w_copies[c]:
            copy.wait()

        kv = nt_dot(normed[...], wkv[:, cols])
        for o in range(2):
            part = kv[:, o * LANES : (o + 1) * LANES]
            if c == 0:
                acc[o, :, q_width:] = part
            else:
                acc[o, :, q_width:] += part

        def query_tiles(half, c=c, cols=cols):
            @pl.loop(0, q_width // 256)
            def _(i):
                at = pl.ds(pl.multiple_of(i * 256, 256), 256)
                part = nt_dot(normed[...], wq[half, at, cols])
                if c == 0:
                    acc[half, :, at] = part
                else:
                    acc[half, :, at] += part

        query_tiles(other)
        if c == Q_CHUNKS - 1:
            push(acc.at[other], acc_in, rs_sem.at[0], rr_sem.at[0], {"col": other})
        query_tiles(col)

    for p in range(8):
        piece = gath[p, :, pl.ds(pl.multiple_of(me * out_width, out_width), out_width)].astype(f32)
        for step in range(2):
            resid[step * 16 + p * 2 : step * 16 + p * 2 + 2, :] = piece[step * 2 : step * 2 + 2]

    landed(acc_in, rr_sem.at[0])
    total = (acc[col] + acc_in[...]).astype(bf16)
    stack = [total[:, j * LANES : (j + 1) * LANES] for j in range(7)]
    stack.append(jnp.zeros((32, LANES), bf16))
    a2a_out[...] = nn_dot(perm_q[...], jnp.concatenate(stack, axis=0)).astype(bf16)
    for i, peer in enumerate(peers):
        push(
            a2a_out.at[pl.ds(pl.multiple_of(peer * 32, 32), 32), :],
            a2a_in.at[me],
            as_sem.at[i],
            ar_sem.at[me],
            {"row": peer},
        )
    a2a_in[me] = a2a_out[pl.ds(pl.multiple_of(me * 32, 32), 32), :]
    for peer in peers:
        landed(a2a_in.at[peer], ar_sem.at[peer])

    news = jnp.concatenate([a2a_in[p, 16:32, :] for p in range(8)], axis=1)
    news = nn_dot(news, spread[...]).astype(bf16)
    for g in range(kv_heads):
        kext[g, 2 * slots : 2 * slots + 16, :] = news[:, g * LANES : (g + 1) * LANES]
        vext[g, 2 * slots : 2 * slots + 16, :] = news[
            :, (kv_heads + g) * LANES : (kv_heads + g + 1) * LANES
        ]
    for p in range(8):
        q32[p * 24 : (p + 1) * 24, :] = a2a_in[p].astype(f32)[0:24]

    def heads_view(g):
        return lambda peer: ag.at[peer, pl.ds(g * 64, 64), :]

    for g in range(kv_heads):
        scores = nt_dot(q32[g * 64 : (g + 1) * 64, :].astype(bf16), kext[g]) * (LANES ** -0.5)
        scores = scores + mask[...]
        exps = jnp.exp(scores - jnp.max(scores, axis=1, keepdims=True))
        probs = (exps / jnp.sum(exps, axis=1, keepdims=True)).astype(bf16)
        result = nn_dot(probs, vext[g])
        result = jnp.where(exits > LAYER_AT, result, 0.0)
        ag[me, g * 64 : (g + 1) * 64, :] = result.astype(bf16)
        spread_own(heads_view(g), g, hs_sem, hr_sem)

    forward(heads_view(0), 0, hs_sem, hr_sem)
    for g in range(kv_heads):
        if g + 1 < kv_heads:
            forward(heads_view(g + 1), g + 1, hs_sem, hr_sem)
        collect(heads_view(g), g, hr_sem)
        for block in range(2):
            at = g * 64 + block * 32
            rows = ag[:, at : at + 32, :].reshape(256, LANES)
            tiles = nn_dot(perm_a[...], rows).astype(bf16)
            for j in range(8):
                lanes = (block * 8 + j) * LANES
                att[:, lanes : lanes + LANES] = tiles[j * 32 : (j + 1) * 32, :]
        for copy in o_copies[g]:
            copy.wait()

        def out_tiles(half, g=g):
            @pl.loop(0, out_width // 256)
            def _(i):
                at = pl.ds(pl.multiple_of(i * 256, 256), 256)
                part = nt_dot(att[...], wo[half, at, pl.ds(g * o_chunk, o_chunk)])
                if g == 0:
                    acc2[half, :, at] = part
                else:
                    acc2[half, :, at] += part

        out_tiles(other)
        if g == kv_heads - 1:
            push(acc2.at[other], acc2_in, rs_sem.at[1], rr_sem.at[1], {"col": other})
        out_tiles(col)
    resid[...] += acc2[col]
    landed(acc2_in, rr_sem.at[1])
    final = (resid[...] + acc2_in[...]).astype(bf16)
    for step in range(2):
        out[step] = final[step * 16 : (step + 1) * 16, :]
    for copy in sends:
        copy.wait_send()


def fused(
    states,
    norm_gain,
    w_query,
    w_key,
    w_value,
    w_out,
    key_cache,
    value_cache,
    cache_len,
    slot_row,
    exit_layer,
):
    steps, own_rows, _, half_width = states.shape
    kv_heads = key_cache.shape[2]
    slots = key_cache.shape[1]
    q_width = w_query.shape[2]
    out_width = w_out.shape[2]
    head_width = w_out.shape[3]
    any_space = pl.BlockSpec(memory_space=pl.ANY)
    vmem = pl.BlockSpec(memory_space=pltpu.VMEM)
    smem = pl.BlockSpec(memory_space=pltpu.SMEM)
    f32 = jnp.float32
    bf16 = jnp.bfloat16
    keys = 2 * slots + LANES
    dma = pltpu.SemaphoreType.DMA
    result = pl.pallas_call(
        fused_kernel,
        out_shape=jax.ShapeDtypeStruct((steps, 16, out_width), bf16),
        in_specs=[any_space, vmem] + [any_space] * 6 + [smem] * 3,
        out_specs=vmem,
        scratch_shapes=[
            pltpu.VMEM((8, steps * own_rows, half_width), bf16),
            pltpu.VMEM((2, q_width, half_width), bf16),
            pltpu.VMEM((2 * LANES, half_width), bf16),
            pltpu.VMEM((2, out_width, head_width), bf16),
            pltpu.VMEM((own_rows, kv_heads, slots, LANES), bf16),
            pltpu.VMEM((own_rows, kv_heads, slots, LANES), bf16),
            pltpu.VMEM((kv_heads, keys, LANES), bf16),
            pltpu.VMEM((kv_heads, keys, LANES), bf16),
            pltpu.VMEM((8, LANES), f32),
            pltpu.VMEM((8, LANES), f32),
            pltpu.VMEM((8, 8, LANES), f32),
            pltpu.VMEM((steps, own_rows, half_width), bf16),
            pltpu.VMEM((steps * own_rows, half_width), f32),
            pltpu.VMEM((32, half_width // Q_CHUNKS), f32),
            pltpu.VMEM((32, half_width // Q_CHUNKS), bf16),
            pltpu.VMEM((2, 32, q_width + LANES), f32),
            pltpu.VMEM((32, q_width + LANES), f32),
            pltpu.VMEM((256, LANES), bf16),
            pltpu.VMEM((8, 32, LANES), bf16),
            pltpu.VMEM((192, LANES), f32),
            pltpu.VMEM((8, 192, LANES), bf16),
            pltpu.VMEM((32, head_width // kv_heads), bf16),
            pltpu.VMEM((2, 32, out_width), f32),
            pltpu.VMEM((32, out_width), f32),
            pltpu.VMEM((32, out_width), f32),
            pltpu.VMEM((256, 256), bf16),
            pltpu.VMEM((256, 256), bf16),
            pltpu.VMEM((8 * LANES, 6 * LANES), bf16),
            pltpu.VMEM((64, keys), f32),
            dma,
            dma((Q_CHUNKS, 6)),
            dma((kv_heads, 2)),
            dma((2,)),
            dma((Q_CHUNKS, 7)),
            dma((Q_CHUNKS, 8)),
            dma((8,)),
            dma((9,)),
            dma((2,)),
            dma((2,)),
            dma((7,)),
            dma((8,)),
            dma((kv_heads, 7)),
            dma((kv_heads, 8)),
        ],
        compiler_params=pltpu.CompilerParams(
            collective_id=0, has_side_effects=True, vmem_limit_bytes=63 * 1024 * 1024
        ),
        name="fused_layer",
    )(
        states.transpose(0, 2, 1, 3)[:, 0],
        norm_gain,
        w_query,
        w_key,
        w_value,
        w_out,
        key_cache.transpose(0, 2, 1, 3),
        value_cache.transpose(0, 2, 1, 3),
        cache_len,
        slot_row,
        exit_layer,
    )
    return result[:, :, None, :]


def on_device_any(*args):
    states, _, w_query, w_key, _, w_out, key_cache = args[:7]
    fits = (
        lax.axis_size("row") == 8
        and lax.axis_size("col") == 2
        and states.shape[:2] == (2, 2)
        and w_query.shape[1:3] == (2, 6 * LANES)
        and w_key.shape[2] == 48
        and key_cache.shape[2:] == (3, LANES)
        and w_out.shape[3] == 48 * LANES
    )
    return fused(*args) if fits else on_device(*args)


def solution(mesh):
    return jax.shard_map(
        on_device_any,
        mesh=mesh,
        in_specs=(
            P(None, ("groups", "row"), "col", None),
            P("col", None),
            P("col", None, "row", None),
            P("col", None, "row", None),
            P("col", None, "row", None),
            P("col", None, "row", None),
            P(("groups", "row"), None, "col", None),
            P(("groups", "row"), None, "col", None),
            P(("groups", "row")),
            P("groups"),
            P(None, "groups"),
        ),
        out_specs=P(None, "groups", "col", "row"),
        check_vma=False,
    )
```

```python
import functools

import jax
import jax.numpy as jnp
from jax import lax
from jax.experimental import pallas as pl
from jax.experimental.pallas import tpu as pltpu
from jax.sharding import PartitionSpec as P

LAYER_AT = 63


epsilon = 1e-05


def on_device(
    states,
    norm_gain,
    w_query,
    w_key,
    w_value,
    w_out,
    key_cache,
    value_cache,
    cache_len,
    slot_row,
    exit_layer,
):
    row_count = lax.axis_size("row")
    row_index = lax.axis_index("row")
    own_rows = key_cache.shape[0]
    half_width = states.shape[3]
    model_width = half_width * w_query.shape[1]
    kv_local = key_cache.shape[2]
    head_size = key_cache.shape[3]
    group_size = w_query.shape[2] * row_count // (kv_local * head_size)
    piece_width = w_out.shape[2]
    scale_factor = head_size ** (-0.5)
    cache_slots = key_cache.shape[1]
    step_total = states.shape[0]
    valid_mask = jnp.arange(cache_slots)[None, :] < cache_len[:, None]
    own_slots = lax.dynamic_slice_in_dim(slot_row, row_index * own_rows, own_rows)
    gain_local = norm_gain[None]
    block_size = 1
    new_keys = []
    new_values = []
    results = []
    for first_step in range(0, step_total, block_size):
        block = states[first_step : first_step + block_size]
        gathered = lax.all_gather(block, "row", axis=1, tiled=True)
        widened = gathered.astype(jnp.float32)
        squares = jnp.sum(jnp.square(widened), axis=3)
        totals = lax.psum(squares, "col")
        scaling = lax.rsqrt(totals / model_width + epsilon)
        normed = (widened * scaling[..., None] * gain_local).astype(jnp.bfloat16)[:, :, 0, :]
        query_part = jnp.einsum(
            "srd,hcd->srhc", normed, w_query[0], preferred_element_type=jnp.float32
        )
        key_part = jnp.einsum("srd,hcd->srhc", normed, w_key[0], preferred_element_type=jnp.float32)
        value_part = jnp.einsum(
            "srd,hcd->srhc", normed, w_value[0], preferred_element_type=jnp.float32
        )
        query_sum, key_sum, value_sum = (
            lax.psum_scatter(query_part, "col", scatter_dimension=2, tiled=True),
            lax.psum_scatter(key_part, "col", scatter_dimension=2, tiled=True),
            lax.psum_scatter(value_part, "col", scatter_dimension=2, tiled=True),
        )
        query_sorted = jnp.take(query_sum.astype(jnp.bfloat16), slot_row, axis=1)
        key_sorted = jnp.take(key_sum.astype(jnp.bfloat16), slot_row, axis=1)
        value_sorted = jnp.take(value_sum.astype(jnp.bfloat16), slot_row, axis=1)
        query_own, key_own, value_own = (
            lax.all_to_all(query_sorted, "row", split_axis=1, concat_axis=3, tiled=True),
            lax.all_to_all(key_sorted, "row", split_axis=1, concat_axis=3, tiled=True),
            lax.all_to_all(value_sorted, "row", split_axis=1, concat_axis=3, tiled=True),
        )
        queries = query_own[0].reshape(own_rows, kv_local, group_size, head_size)
        new_keys.append(key_own[0].reshape(own_rows, kv_local, head_size))
        new_values.append(value_own[0].reshape(own_rows, kv_local, head_size))
        cache_scores = (
            jnp.einsum("bghd,blgd->bghl", queries, key_cache, preferred_element_type=jnp.float32)
            * scale_factor
        )
        cache_scores = jnp.where(valid_mask[:, None, None, :], cache_scores, -jnp.inf)
        fresh_scores = (
            jnp.stack(
                [
                    jnp.einsum(
                        "bghd,bgd->bgh", queries, earlier, preferred_element_type=jnp.float32
                    )
                    for earlier in new_keys
                ],
                axis=-1,
            )
            * scale_factor
        )
        largest = jnp.maximum(jnp.max(cache_scores, axis=-1), jnp.max(fresh_scores, axis=-1))
        cache_exps = jnp.exp(cache_scores - largest[..., None])
        fresh_exps = jnp.exp(fresh_scores - largest[..., None])
        denominator = jnp.sum(cache_exps, axis=-1) + jnp.sum(fresh_exps, axis=-1)
        weights_cache = (cache_exps / denominator[..., None]).astype(jnp.bfloat16)
        weights_fresh = (fresh_exps / denominator[..., None]).astype(jnp.bfloat16)
        attended = jnp.einsum(
            "bghl,blgd->bghd", weights_cache, value_cache, preferred_element_type=jnp.float32
        )
        attended = attended + jnp.einsum(
            "bght,btgd->bghd",
            weights_fresh,
            jnp.stack(new_values, axis=1),
            preferred_element_type=jnp.float32,
        )
        active = jnp.take(exit_layer[first_step], own_slots) > LAYER_AT
        attended = (
            jnp.where(active[:, None, None, None], attended, 0.0)
            .astype(jnp.bfloat16)
            .reshape(own_rows, -1)
        )
        attended_block = [attended]
        attended_all = jnp.stack(attended_block)
        projection_terms = jnp.einsum(
            "srf,hcf->srhc",
            lax.all_gather(attended_all, "row", axis=1, tiled=True),
            w_out[0],
            preferred_element_type=jnp.float32,
        )
        projected = lax.psum_scatter(projection_terms, "col", scatter_dimension=2, tiled=True)
        reordered = jnp.zeros_like(projected).at[:, slot_row].set(projected)
        residual = lax.dynamic_slice_in_dim(
            gathered, row_index * piece_width, piece_width, 3
        ).astype(jnp.float32)
        results.append((residual + reordered).astype(jnp.bfloat16))
    return jnp.concatenate(results, axis=0)


MESH = pl.DeviceIdType.MESH
LANES = 128
Q_CHUNKS = 4
NEG = float("-inf")


def nt_dot(a, b):
    return lax.dot_general(a, b, (((1,), (1,)), ((), ())), preferred_element_type=jnp.float32)


def nn_dot(a, b):
    return lax.dot_general(a, b, (((1,), (0,)), ((), ())), preferred_element_type=jnp.float32)


def fused_kernel(
    states,
    gain,
    w_query,
    w_key,
    w_value,
    w_out,
    key_cache,
    value_cache,
    cache_len,
    slot_row,
    exit_layer,
    out,
    gath,
    wq,
    wkv,
    wo,
    kc,
    vc,
    kext,
    vext,
    sums_own,
    sums_in,
    sums_all,
    own_rows,
    own32,
    norm32,
    normed,
    acc,
    acc_in,
    a2a_out,
    a2a_in,
    q32,
    ag,
    att,
    acc2,
    acc2_in,
    resid,
    perm_q,
    perm_a,
    spread,
    mask,
    own_sem,
    wq_sem,
    wo_sem,
    cache_sem,
    gs_sem,
    gr_sem,
    ss_sem,
    sr_sem,
    rs_sem,
    rr_sem,
    as_sem,
    ar_sem,
    hs_sem,
    hr_sem,
):
    me = lax.axis_index("row")
    col = lax.axis_index("col")
    other = 1 - col
    x = lax.rem(me, 2)
    z = lax.div(me, 2)
    beside = me + 1 - 2 * x
    along = [lax.rem(z + d, 4) * 2 + x for d in (1, 2, 3)]
    across = [lax.rem(z + d, 4) * 2 + 1 - x for d in (0, 1, 2, 3)]
    peers = [lax.rem(me + d, 8) for d in range(1, 8)]
    half_width = gath.shape[2]
    model_width = half_width * 2
    k_chunk = half_width // Q_CHUNKS
    q_width = wq.shape[1]
    kv_width = w_key.shape[2]
    out_width = wo.shape[1]
    kv_heads = kext.shape[0]
    slots = kc.shape[2]
    o_chunk = wo.shape[2] // kv_heads
    f32 = jnp.float32
    bf16 = jnp.bfloat16

    own = pltpu.make_async_copy(states, own_rows, own_sem)
    own.start()
    w_copies = []
    for c in range(Q_CHUNKS):
        cols = pl.ds(c * k_chunk, k_chunk)
        group = []
        for o in range(2):
            group.append((w_query.at[0, o, :, cols], wq.at[o, :, cols]))
            group.append((w_key.at[0, o, :, cols], wkv.at[pl.ds(o * LANES, kv_width), cols]))
            group.append(
                (w_value.at[0, o, :, cols], wkv.at[pl.ds(o * LANES + kv_width, kv_width), cols])
            )
        w_copies.append(
            [
                pltpu.make_async_copy(src, dst, wq_sem.at[c, i])
                for i, (src, dst) in enumerate(group)
            ]
        )
    o_copies = []
    for g in range(kv_heads):
        cols = pl.ds(g * o_chunk, o_chunk)
        o_copies.append(
            [
                pltpu.make_async_copy(w_out.at[0, o, :, cols], wo.at[o, :, cols], wo_sem.at[g, o])
                for o in range(2)
            ]
        )
    c_copies = [
        pltpu.make_async_copy(key_cache, kc, cache_sem.at[0]),
        pltpu.make_async_copy(value_cache, vc, cache_sem.at[1]),
    ]
    for copy in w_copies[0] + c_copies:
        copy.start(priority=1)
    for group in w_copies[1:]:
        for copy in group:
            copy.start(priority=1)

    barrier = pltpu.get_barrier_semaphore()
    for peer in peers:
        pl.semaphore_signal(barrier, inc=1, device_id={"row": peer}, device_id_type=MESH)
    pl.semaphore_signal(barrier, inc=1, device_id={"col": other}, device_id_type=MESH)
    pl.semaphore_wait(barrier, 8)

    sends = []

    def push(src, dst, send_sem, recv_sem, where):
        copy = pltpu.make_async_remote_copy(
            src_ref=src,
            dst_ref=dst,
            send_sem=send_sem,
            recv_sem=recv_sem,
            device_id=where,
            device_id_type=MESH,
        )
        copy.start()
        sends.append(copy)

    def landed(ref, recv_sem):
        pltpu.make_async_remote_copy(
            src_ref=ref,
            dst_ref=ref,
            send_sem=own_sem,
            recv_sem=recv_sem,
            device_id={"row": beside},
            device_id_type=MESH,
        ).wait_recv()

    def spread_own(view, c, send_sem, recv_sem):
        push(view(me), view(me), send_sem.at[c, 0], recv_sem.at[c, me], {"row": beside})
        for i, peer in enumerate(along):
            push(view(me), view(me), send_sem.at[c, 1 + i], recv_sem.at[c, me], {"row": peer})

    def forward(view, c, send_sem, recv_sem):
        for i, peer in enumerate(along):
            landed(view(peer), recv_sem.at[c, peer])
            push(view(peer), view(peer), send_sem.at[c, 4 + i], recv_sem.at[c, peer], {"row": beside})

    def collect(view, c, recv_sem):
        for peer in across:
            landed(view(peer), recv_sem.at[c, peer])

    def state_view(c):
        return lambda peer: gath.at[peer, :, pl.ds(c * k_chunk, k_chunk)]

    own.wait()
    for step in range(2):
        own32[step * 2 : step * 2 + 2, :] = own_rows[step].astype(f32)
    gath[me] = own32[...].astype(bf16)
    for c in range(Q_CHUNKS):
        spread_own(state_view(c), c, gs_sem, gr_sem)

    mine = own32[...]
    square = jnp.sum(mine * mine, axis=1, keepdims=True)
    sums_own[0:4, :] = jnp.broadcast_to(square, (4, LANES))
    sums_own[4:8, :] = jnp.zeros((4, LANES), f32)
    push(sums_own, sums_in, ss_sem.at[0], sr_sem.at[8], {"col": other})
    landed(sums_in, sr_sem.at[8])
    sums_all[me] = sums_own[...] + sums_in[...]
    for i, peer in enumerate(peers):
        push(sums_all.at[me], sums_all.at[me], ss_sem.at[1 + i], sr_sem.at[me], {"row": peer})

    for o in range(2):
        wkv[pl.ds(o * LANES + 2 * kv_width, LANES - 2 * kv_width), :] = jnp.zeros(
            (LANES - 2 * kv_width, half_width), bf16
        )
    r = lax.broadcasted_iota(jnp.int32, (256, 1), 0)
    slot_of = (r >> 5) * 2 + (r & 1)
    target = jnp.zeros((256, 1), jnp.int32)
    for t in range(16):
        target = jnp.where(slot_of == t, slot_row[t], target)
    q = lax.broadcasted_iota(jnp.int32, (256, 256), 1)
    row_of = ((q >> 2) & 7) * 2 + (q & 1)
    hit = (((r >> 2) & 7) == (q >> 5)) & (((r >> 1) & 1) == ((q >> 1) & 1)) & (row_of == target)
    perm_q[...] = jnp.where(hit, 1.0, 0.0).astype(bf16)
    q = lax.broadcasted_iota(jnp.int32, (1, 256), 1)
    slot_of = (q >> 5) * 2 + (q & 1)
    target = jnp.zeros((1, 256), jnp.int32)
    for t in range(16):
        target = jnp.where(slot_of == t, slot_row[t], target)
    r = lax.broadcasted_iota(jnp.int32, (256, 256), 0)
    hit = (((q >> 2) & 7) == (r >> 5)) & (((q >> 1) & 1) == ((r >> 4) & 1)) & ((r & 15) == target)
    perm_a[...] = jnp.where(hit, 1.0, 0.0).astype(bf16)
    n = lax.broadcasted_iota(jnp.int32, (LANES, 6 * LANES), 1)
    lane = lax.broadcasted_iota(jnp.int32, (LANES, 6 * LANES), 0)
    place = jnp.where(lane < kv_width, lane, lane - kv_width + 3 * LANES)
    place = jnp.where(lane < 2 * kv_width, place, -10000)
    for p in range(8):
        spread[p * LANES : (p + 1) * LANES, :] = jnp.where(
            n == place + p * kv_width, 1.0, 0.0
        ).astype(bf16)
    r = lax.broadcasted_iota(jnp.int32, mask.shape, 0)
    k = lax.broadcasted_iota(jnp.int32, mask.shape, 1)
    b = r & 1
    s = (r >> 1) & 1
    f = k - 2 * slots - 8
    limit = b * slots + jnp.where(b == 0, cache_len[0], cache_len[1])
    cached = (k >= b * slots) & (k < limit)
    fresh = (f >= 0) & (f < 4) & ((f & 1) == b) & ((f >> 1) <= s)
    mask[...] = jnp.where(cached | fresh, 0.0, NEG)
    r = lax.broadcasted_iota(jnp.int32, (64, LANES), 0) & 3
    exits = jnp.zeros((64, LANES), jnp.int32)
    for step in range(2):
        for slot in range(2):
            layer = exit_layer[step, slot_row[me * 2 + slot]]
            exits = jnp.where(r == step * 2 + slot, layer, exits)

    def stage_caches():
        for copy in c_copies:
            copy.wait()
        for slot in range(2):
            for g in range(kv_heads):
                kext[g, slot * slots : (slot + 1) * slots, :] = kc[slot, g]
                vext[g, slot * slots : (slot + 1) * slots, :] = vc[slot, g]
        for g in range(kv_heads):
            kext[g, 2 * slots :, :] = jnp.zeros((LANES, LANES), bf16)
            vext[g, 2 * slots :, :] = jnp.zeros((LANES, LANES), bf16)

    forward(state_view(0), 0, gs_sem, gr_sem)
    stage_caches()
    for peer in peers:
        landed(sums_all.at[peer], sr_sem.at[peer])
    scale = [
        lax.rsqrt(sums_all[p, 0:4, 0:1] / model_width + epsilon) for p in range(8)
    ]
    for c in range(Q_CHUNKS):
        cols = pl.ds(c * k_chunk, k_chunk)
        if c + 1 < Q_CHUNKS:
            forward(state_view(c + 1), c + 1, gs_sem, gr_sem)
        collect(state_view(c), c, gr_sem)
        if c >= 1:
            for copy in o_copies[c - 1]:
                copy.start(priority=1)
        for p in range(8):
            norm32[p * 4 : (p + 1) * 4, :] = (
                gath[p, :, cols].astype(f32) * scale[p] * gain[:, cols]
            )
        normed[...] = norm32[...].astype(bf16)
        for copy in w_copies[c]:
            copy.wait()

        kv = nt_dot(normed[...], wkv[:, cols])
        for o in range(2):
            part = kv[:, o * LANES : (o + 1) * LANES]
            if c == 0:
                acc[o, :, q_width:] = part
            else:
                acc[o, :, q_width:] += part

        def query_tiles(half, c=c, cols=cols):
            @pl.loop(0, q_width // 256, unroll=True)
            def _(i):
                at = pl.ds(pl.multiple_of(i * 256, 256), 256)
                part = nt_dot(normed[...], wq[half, at, cols])
                if c == 0:
                    acc[half, :, at] = part
                else:
                    acc[half, :, at] += part

        query_tiles(other)
        if c == Q_CHUNKS - 1:
            push(acc.at[other], acc_in, rs_sem.at[0], rr_sem.at[0], {"col": other})
        query_tiles(col)

    for p in range(8):
        piece = gath[p, :, pl.ds(pl.multiple_of(me * out_width, out_width), out_width)].astype(f32)
        for step in range(2):
            resid[step * 16 + p * 2 : step * 16 + p * 2 + 2, :] = piece[step * 2 : step * 2 + 2]

    landed(acc_in, rr_sem.at[0])
    total = (acc[col] + acc_in[...]).astype(bf16)
    stack = [total[:, j * LANES : (j + 1) * LANES] for j in range(7)]
    stack.append(jnp.zeros((32, LANES), bf16))
    a2a_out[...] = nn_dot(perm_q[...], jnp.concatenate(stack, axis=0)).astype(bf16)
    for i, peer in enumerate(peers):
        push(
            a2a_out.at[pl.ds(pl.multiple_of(peer * 32, 32), 32), :],
            a2a_in.at[me],
            as_sem.at[i],
            ar_sem.at[me],
            {"row": peer},
        )
    a2a_in[me] = a2a_out[pl.ds(pl.multiple_of(me * 32, 32), 32), :]
    for peer in peers:
        landed(a2a_in.at[peer], ar_sem.at[peer])

    news = jnp.concatenate([a2a_in[p, 16:32, :] for p in range(8)], axis=1)
    news = nn_dot(news, spread[...]).astype(bf16)
    for g in range(kv_heads):
        kext[g, 2 * slots : 2 * slots + 16, :] = news[:, g * LANES : (g + 1) * LANES]
        vext[g, 2 * slots : 2 * slots + 16, :] = news[
            :, (kv_heads + g) * LANES : (kv_heads + g + 1) * LANES
        ]
    for p in range(8):
        q32[p * 24 : (p + 1) * 24, :] = a2a_in[p].astype(f32)[0:24]

    def heads_view(g):
        return lambda peer: ag.at[peer, pl.ds(g * 64, 64), :]

    for g in range(kv_heads):
        scores = nt_dot(q32[g * 64 : (g + 1) * 64, :].astype(bf16), kext[g]) * (LANES ** -0.5)
        scores = scores + mask[...]
        exps = jnp.exp(scores - jnp.max(scores, axis=1, keepdims=True))
        probs = (exps / jnp.sum(exps, axis=1, keepdims=True)).astype(bf16)
        result = nn_dot(probs, vext[g])
        result = jnp.where(exits > LAYER_AT, result, 0.0)
        ag[me, g * 64 : (g + 1) * 64, :] = result.astype(bf16)
        spread_own(heads_view(g), g, hs_sem, hr_sem)

    forward(heads_view(0), 0, hs_sem, hr_sem)
    for g in range(kv_heads):
        if g + 1 < kv_heads:
            forward(heads_view(g + 1), g + 1, hs_sem, hr_sem)
        collect(heads_view(g), g, hr_sem)
        for block in range(2):
            at = g * 64 + block * 32
            rows = ag[:, at : at + 32, :].reshape(256, LANES)
            tiles = nn_dot(perm_a[...], rows).astype(bf16)
            for j in range(8):
                lanes = (block * 8 + j) * LANES
                att[:, lanes : lanes + LANES] = tiles[j * 32 : (j + 1) * 32, :]
        for copy in o_copies[g]:
            copy.wait()

        def out_tiles(half, g=g):
            @pl.loop(0, out_width // 256, unroll=True)
            def _(i):
                at = pl.ds(pl.multiple_of(i * 256, 256), 256)
                part = nt_dot(att[...], wo[half, at, pl.ds(g * o_chunk, o_chunk)])
                if g == 0:
                    acc2[half, :, at] = part
                else:
                    acc2[half, :, at] += part

        out_tiles(other)
        if g == kv_heads - 1:
            push(acc2.at[other], acc2_in, rs_sem.at[1], rr_sem.at[1], {"col": other})
        out_tiles(col)
    resid[...] += acc2[col]
    landed(acc2_in, rr_sem.at[1])
    final = (resid[...] + acc2_in[...]).astype(bf16)
    for step in range(2):
        out[step] = final[step * 16 : (step + 1) * 16, :]
    for copy in sends:
        copy.wait_send()


def fused(
    states,
    norm_gain,
    w_query,
    w_key,
    w_value,
    w_out,
    key_cache,
    value_cache,
    cache_len,
    slot_row,
    exit_layer,
):
    steps, own_rows, _, half_width = states.shape
    kv_heads = key_cache.shape[2]
    slots = key_cache.shape[1]
    q_width = w_query.shape[2]
    out_width = w_out.shape[2]
    head_width = w_out.shape[3]
    any_space = pl.BlockSpec(memory_space=pl.ANY)
    vmem = pl.BlockSpec(memory_space=pltpu.VMEM)
    smem = pl.BlockSpec(memory_space=pltpu.SMEM)
    f32 = jnp.float32
    bf16 = jnp.bfloat16
    keys = 2 * slots + LANES
    dma = pltpu.SemaphoreType.DMA
    result = pl.pallas_call(
        fused_kernel,
        out_shape=jax.ShapeDtypeStruct((steps, 16, out_width), bf16),
        in_specs=[any_space, vmem] + [any_space] * 6 + [smem] * 3,
        out_specs=vmem,
        scratch_shapes=[
            pltpu.VMEM((8, steps * own_rows, half_width), bf16),
            pltpu.VMEM((2, q_width, half_width), bf16),
            pltpu.VMEM((2 * LANES, half_width), bf16),
            pltpu.VMEM((2, out_width, head_width), bf16),
            pltpu.VMEM((own_rows, kv_heads, slots, LANES), bf16),
            pltpu.VMEM((own_rows, kv_heads, slots, LANES), bf16),
            pltpu.VMEM((kv_heads, keys, LANES), bf16),
            pltpu.VMEM((kv_heads, keys, LANES), bf16),
            pltpu.VMEM((8, LANES), f32),
            pltpu.VMEM((8, LANES), f32),
            pltpu.VMEM((8, 8, LANES), f32),
            pltpu.VMEM((steps, own_rows, half_width), bf16),
            pltpu.VMEM((steps * own_rows, half_width), f32),
            pltpu.VMEM((32, half_width // Q_CHUNKS), f32),
            pltpu.VMEM((32, half_width // Q_CHUNKS), bf16),
            pltpu.VMEM((2, 32, q_width + LANES), f32),
            pltpu.VMEM((32, q_width + LANES), f32),
            pltpu.VMEM((256, LANES), bf16),
            pltpu.VMEM((8, 32, LANES), bf16),
            pltpu.VMEM((192, LANES), f32),
            pltpu.VMEM((8, 192, LANES), bf16),
            pltpu.VMEM((32, head_width // kv_heads), bf16),
            pltpu.VMEM((2, 32, out_width), f32),
            pltpu.VMEM((32, out_width), f32),
            pltpu.VMEM((32, out_width), f32),
            pltpu.VMEM((256, 256), bf16),
            pltpu.VMEM((256, 256), bf16),
            pltpu.VMEM((8 * LANES, 6 * LANES), bf16),
            pltpu.VMEM((64, keys), f32),
            dma,
            dma((Q_CHUNKS, 6)),
            dma((kv_heads, 2)),
            dma((2,)),
            dma((Q_CHUNKS, 7)),
            dma((Q_CHUNKS, 8)),
            dma((8,)),
            dma((9,)),
            dma((2,)),
            dma((2,)),
            dma((7,)),
            dma((8,)),
            dma((kv_heads, 7)),
            dma((kv_heads, 8)),
        ],
        compiler_params=pltpu.CompilerParams(
            collective_id=0, has_side_effects=True, vmem_limit_bytes=63 * 1024 * 1024
        ),
        name="fused_layer",
    )(
        states.transpose(0, 2, 1, 3)[:, 0],
        norm_gain,
        w_query,
        w_key,
        w_value,
        w_out,
        key_cache.transpose(0, 2, 1, 3),
        value_cache.transpose(0, 2, 1, 3),
        cache_len,
        slot_row,
        exit_layer,
    )
    return result[:, :, None, :]


def on_device_any(*args):
    states, _, w_query, w_key, _, w_out, key_cache = args[:7]
    fits = (
        lax.axis_size("row") == 8
        and lax.axis_size("col") == 2
        and states.shape[:2] == (2, 2)
        and w_query.shape[1:3] == (2, 6 * LANES)
        and w_key.shape[2] == 48
        and key_cache.shape[2:] == (3, LANES)
        and w_out.shape[3] == 48 * LANES
    )
    return fused(*args) if fits else on_device(*args)


def solution(mesh):
    return jax.shard_map(
        on_device_any,
        mesh=mesh,
        in_specs=(
            P(None, ("groups", "row"), "col", None),
            P("col", None),
            P("col", None, "row", None),
            P("col", None, "row", None),
            P("col", None, "row", None),
            P("col", None, "row", None),
            P(("groups", "row"), None, "col", None),
            P(("groups", "row"), None, "col", None),
            P(("groups", "row")),
            P("groups"),
            P(None, "groups"),
        ),
        out_specs=P(None, "groups", "col", "row"),
        check_vma=False,
    )
```
